32 devices in a mesh: blk: 16 (over z, x, core), rep: 2 (over y).
Axes of the slice: x: 2, y: 2, z: 4, core: 2. Of those that a mesh axis runs over, the one named last changes fastest.
Arguments:
- features: bfloat16 [4096, 256], P('blk'), may hold values from -6 to 6
- degree: int32 [4096], P('blk'), may hold values from 1 to 4
- tiles: bfloat16 [16, 2, 16, 8, 128, 128], P('blk', 'rep'), may hold values from -0.0625 to 0.0625
- block_rows: int32 [16, 2, 16, 8], P('blk', 'rep'), may hold values from 0 to 1
- block_cols: int32 [16, 2, 16, 8], P('blk', 'rep'), may hold values from 0 to 1
- live: int32 [16, 2, 16], P('blk', 'rep'), may hold values from 1 to 8, as said below
- w_self: bfloat16 [256, 256], replicated, may hold values from -0.375 to 0.375
- w_neigh: bfloat16 [256, 256], replicated, may hold values from -0.375 to 0.375
- bias: float32 [256], replicated, may hold values from -3 to 3
- cotangent: bfloat16 [4096, 256], P('blk'), may hold values from -1 to 1
Outputs:
- hidden_out: bfloat16 [4096, 256], P(('blk', 'rep'))
- feature_grad: bfloat16 [4096, 256], P(('blk', 'rep'))
- grad_self: float32 [256, 256], replicated
- grad_neigh: float32 [256, 256], replicated
- grad_bias: float32 [256], replicated
The draws below stay inside these ranges and needn't reach their ends.
Inputs may be any that keep to these rules, and one draw needn't show every extreme that they name: `live`: each device's slots for one column slab are used from slot 0 on; at most 8, and exactly 8 for some device and slab.
All inputs are finite; a program needn't handle non-finite values.
Results may differ from the reference program's by a relative error of at most 0.0095.
Values may be sent and summed in bfloat16 or wider, within the bound.
A program may use at most 192 MiB of HBM per device.

```python
import jax
import jax.numpy as jnp
from jax import lax

D = 256
TILE = 128
NB = 2
CAP = 8
NODES = 4096
N_BLK = 16
N_REP = 2


def draw_live(key, part):
    key = jax.random.fold_in(key, 7)
    key_level, key_count, key_spot = jax.random.split(key, 3)
    level = jax.random.randint(key_level, (N_BLK, N_REP, 1), 0, 2)
    ceiling = jnp.maximum(jnp.right_shift(jnp.int32(CAP), level), 1)
    lower = (ceiling + 1) // 2
    counts = jax.random.randint(key_count, (N_BLK, N_REP, N_BLK), lower, ceiling + 1)
    spot = jax.random.randint(key_spot, (), 0, N_BLK * N_REP * N_BLK)
    flat = counts.reshape(-1)
    flat = jnp.where(jnp.arange(N_BLK * N_REP * N_BLK) == spot, CAP, flat)
    return flat.reshape(N_BLK, N_REP, N_BLK).astype(jnp.int32)


def touch_ends(drawn, stream_key, smallest, high):
    spot = [jax.random.randint(jax.random.fold_in(stream_key, axis), (), 0, length) for axis, length in enumerate(drawn.shape)]
    longest = drawn.shape.index(max(drawn.shape))
    next_to = spot[:longest] + [(spot[longest] + 1) % drawn.shape[longest]] + spot[longest + 1:]
    return drawn.at[tuple(spot)].set(smallest).at[tuple(next_to)].set(high)


def block_scale(key, extent, pieces, least, largest):
    def one(axis_at, shards_of):
        steps = jax.random.uniform(jax.random.fold_in(jax.random.fold_in(key, 6), axis_at), (shards_of,), jnp.float32, least / len(pieces), largest / len(pieces))
        return jnp.repeat(jnp.exp(steps), extent[axis_at] // shards_of).reshape((-1,) + (1,) * (len(extent) - axis_at - 1))

    level = one(*pieces[0])
    for cut in pieces[1:]:
        level = level * one(*cut)
    return level


def bell_draw(rng, dims, spread, reach, cuts=(), held_as=jnp.bfloat16):
    values = spread * jax.random.normal(rng, dims, jnp.float32)
    if cuts:
        values = values * block_scale(rng, dims, cuts, -0.22, 0.18)
    return jnp.clip(values, -reach, reach).astype(held_as)


def setup_inputs(seed: int = 0) -> dict:
    keys = jax.random.split(jax.random.key(seed), 11)
    features = bell_draw(keys[0], (NODES, D), 1.0, 6.0, ((0, 16),))
    degree = touch_ends(jax.random.randint(keys[1], (NODES,), 1, 5), jax.random.fold_in(keys[1], 1), 1, 4).astype(jnp.int32)
    tiles = bell_draw(keys[2], (N_BLK, N_REP, N_BLK, CAP, TILE, TILE), (N_BLK * N_REP * CAP * 32) ** -0.5, 0.0625, ((0, 16), (1, 2)))
    block_rows = touch_ends(jax.random.randint(keys[3], (N_BLK, N_REP, N_BLK, CAP), 0, NB), jax.random.fold_in(keys[3], 1), 0, NB - 1).astype(jnp.int32)
    block_cols = touch_ends(jax.random.randint(keys[4], (N_BLK, N_REP, N_BLK, CAP), 0, NB), jax.random.fold_in(keys[4], 1), 0, NB - 1).astype(jnp.int32)
    live = draw_live(jax.random.fold_in(keys[10], 71), 0)
    w_self = bell_draw(keys[6], (D, D), D ** -0.5, 0.375)
    w_neigh = bell_draw(keys[7], (D, D), D ** -0.5, 0.375)
    bias = bell_draw(keys[8], (D,), 0.5, 3.0, (), jnp.float32)
    cotangent = bell_draw(keys[9], (NODES, D), 0.125, 1.0, ((0, 16),))
    return dict(features=features, degree=degree, tiles=tiles, block_rows=block_rows, block_cols=block_cols, live=live, w_self=w_self, w_neigh=w_neigh, bias=bias, cotangent=cotangent)


def silu_slope(pre):
    sig = jax.nn.sigmoid(pre)
    return sig * (1.0 + pre * (1.0 - sig))


def reference(features, degree, tiles, block_rows, block_cols, live, w_self, w_neigh, bias, cotangent):
    nblocks = N_BLK * NB
    blocks_x = features.reshape(nblocks, TILE, D).astype(jnp.float32)
    slot_ids = jnp.arange(CAP, dtype=jnp.int32)
    slab_ids = jnp.arange(N_BLK, dtype=jnp.int32)

    def forward_slab(b):
        tile_b = tiles[b].astype(jnp.float32)
        used = (slot_ids[None, None, :] < live[b][:, :, None]).astype(jnp.float32)
        col_glob = (slab_ids[None, :, None] * NB + block_cols[b]).astype(jnp.int32)
        picked = blocks_x[col_glob] * used[..., None, None]
        prods = jnp.einsum("rsctj,rscjf->rsctf", tile_b, picked)
        total = jnp.zeros((NB, TILE, D), jnp.float32)
        total = total.at[block_rows[b].reshape(-1)].add(prods.reshape(-1, TILE, D))
        return total

    agg_sum = lax.map(forward_slab, slab_ids).reshape(NODES, D)
    degf = degree.astype(jnp.float32)[:, None]
    agg = (agg_sum / degf).astype(jnp.bfloat16)
    pre = (jnp.dot(features, w_self, preferred_element_type=jnp.float32)
           + jnp.dot(agg, w_neigh, preferred_element_type=jnp.float32) + bias)
    hidden_out = jax.nn.silu(pre).astype(jnp.bfloat16)
    dpre = (cotangent.astype(jnp.float32) * silu_slope(pre)).astype(jnp.bfloat16)
    grad_self = jnp.dot(features.T, dpre, preferred_element_type=jnp.float32)
    grad_neigh = jnp.dot(agg.T, dpre, preferred_element_type=jnp.float32)
    grad_bias = jnp.sum(dpre.astype(jnp.float32), axis=0)
    dagg = (jnp.dot(dpre, w_neigh.T, preferred_element_type=jnp.float32) / degf).astype(jnp.bfloat16)
    blocks_g = dagg.reshape(nblocks, TILE, D).astype(jnp.float32)

    def backward_slab(carry, b):
        tile_b = tiles[b].astype(jnp.float32)
        used = (slot_ids[None, None, :] < live[b][:, :, None]).astype(jnp.float32)
        col_glob = (slab_ids[None, :, None] * NB + block_cols[b]).astype(jnp.int32)
        row_glob = (b * NB + block_rows[b]).astype(jnp.int32)
        picked = blocks_g[row_glob] * used[..., None, None]
        prods = jnp.einsum("rscji,rscjf->rscif", tile_b, picked)
        carry = carry.at[col_glob.reshape(-1)].add(prods.reshape(-1, TILE, D))
        return carry, None

    back, _ = lax.scan(backward_slab, jnp.zeros((nblocks, TILE, D), jnp.float32), slab_ids)
    feature_grad = (jnp.dot(dpre, w_self.T, preferred_element_type=jnp.float32)
                    + back.reshape(NODES, D)).astype(jnp.bfloat16)
    return hidden_out, feature_grad, grad_self, grad_neigh, grad_bias
```

```python
import functools

import jax
import jax.numpy as jnp
from jax import lax
from jax.experimental import pallas as pl
from jax.experimental.pallas import tpu as pltpu
from jax.sharding import PartitionSpec as P

BF = jnp.bfloat16
F32 = jnp.float32
MESH = pl.DeviceIdType.MESH
NT = (((1,), (1,)), ((), ()))
ROWS = 16
STRIP = 32


def split_rows(share):
    units = share // ROWS
    side = max(1, units * 3 // 8)
    sizes = [side, units - 2 * side, side]
    orders = ["oir", "iro", "roi"]
    parts, at = [], 0
    for size, order in zip(sizes, orders):
        if size > 0:
            parts.append((at * ROWS, size * ROWS, order))
            at += size
    return parts


def slot_shapes(parts, sizes, width):
    shapes = []
    for _, rows, order in parts:
        left = dict(sizes)
        for axis in reversed(order):
            peers = left.pop(axis) - 1
            shapes.append((peers,) + tuple(left[a] for a in "oir" if a in left) + (rows, width))
    return shapes


class Wire:
    def __init__(self, send, recv):
        self.send, self.recv, self.copies = send, recv, []

    def copy(self, src, dst, device):
        k = len(self.copies)
        c = pltpu.make_async_remote_copy(
            src_ref=src, dst_ref=dst, send_sem=self.send.at[k], recv_sem=self.recv.at[k],
            device_id=device, device_id_type=MESH,
        )
        c.start()
        self.copies.append(c)
        return c


def kernel(
    sizes, parts, nslab, cap, tile, width, slab, share,
    x_ref, deg_ref, tiles_ref, rows_ref, cols_ref, live_ref, ws_ref, wn_ref, bias_ref, cot_ref,
    hid_ref, fg_ref, gs_ref, gn_ref, gb_ref,
    tv, a_v, at_v, xg, part_v, xw, degc, xt, aggp, aggs, aggr, dg, core_in, selfp,
    g_v, g_core, g_in, g_out, g_rep, ga, b_core, b_in, b_out, b_rep,
    send_sem, recv_sem, local_sem, *slots,
):
    n_o, n_i, n_r = sizes["o"], sizes["i"], sizes["r"]
    nb = slab // tile
    blk = lax.axis_index("blk")
    rep = lax.axis_index("rep")
    core = lax.rem(blk, 2)
    sib = 1 - core
    me = {"o": blk // (2 * n_i), "i": lax.rem(blk // 2, n_i), "r": rep}
    wire = Wire(send_sem, recv_sem)

    def device(axis, to):
        at = dict(me)
        at[axis] = to
        return ((at["o"] * n_i + at["i"]) * 2 + core, at["r"])

    sibling = ((me["o"] * n_i + me["i"]) * 2 + sib, rep)

    def peers(axis):
        for k in range(1, sizes[axis]):
            to = lax.rem(me[axis] + k, sizes[axis])
            yield k, to, device(axis, to)

    load = pltpu.make_async_copy(tiles_ref.at[0, 0], tv, local_sem)
    load.start()

    mine = pl.multiple_of(rep * share, share)
    x_mine = x_ref[pl.ds(mine, share), :]
    xg[me["o"], me["i"], core, rep] = x_mine

    barrier = pltpu.get_barrier_semaphore()
    everyone = [sibling] + [d for axis in "oir" for _, _, d in peers(axis)]
    for d in everyone:
        pl.semaphore_signal(barrier, inc=1, device_id=d, device_id_type=MESH)
    pl.semaphore_wait(barrier, len(everyone))

    def box(ref, have, start, rows, core_at, fixed=None):
        at = [slice(None) if a in have else me[a] for a in "oir"]
        if fixed is not None:
            at["oir".index(fixed[0])] = fixed[1]
        return (at[0], at[1], core_at, at[2], pl.ds(start, rows), slice(None))

    def gather_stage(n):
        sent = []
        for start, rows, order in parts:
            at = box(xg, order[:n], start, rows, core)
            sent.append([wire.copy(xg.at[at], xg.at[at], d) for _, _, d in peers(order[n])])
        return sent

    flying = gather_stage(0)

    load.wait()

    def build(s, carry):
        live = live_ref[0, 0, s]
        weights = []
        for c in range(cap):
            row, col = rows_ref[0, 0, s, c], cols_ref[0, 0, s, c]
            used = c < live
            weights.append([
                [jnp.where(used & (row == i) & (col == j), 1.0, 0.0).astype(F32) for j in range(nb)]
                for i in range(nb)
            ])
        for r0 in range(0, tile, STRIP):
            acc = [[jnp.zeros((STRIP, tile), F32) for _ in range(nb)] for _ in range(nb)]
            for c in range(cap):
                t = tv[s, c, r0:r0 + STRIP, :].astype(F32)
                for i in range(nb):
                    for j in range(nb):
                        acc[i][j] = acc[i][j] + t * weights[c][i][j]
            for i in range(nb):
                for j in range(nb):
                    a_v[s, i * tile + r0:i * tile + r0 + STRIP, j * tile:(j + 1) * tile] = acc[i][j].astype(BF)
        at_v[s] = a_v[s].T
        return carry

    half = nslab // 2
    lax.fori_loop(0, half, build, 0)

    for group in flying:
        for c in group:
            c.wait_recv()
    flying = gather_stage(1)

    lax.fori_loop(half, nslab, build, 0)
    xw[...] = jnp.dot(x_mine, ws_ref[...], preferred_element_type=F32)
    xt[...] = x_mine.T
    degf = deg_ref[...].astype(F32).reshape(1, slab)
    degc[...] = jnp.broadcast_to(degf, (128, slab)).T

    for group in flying:
        for c in group:
            c.wait_recv()
    flying = gather_stage(2)
    across = []
    for group, (start, rows, order) in zip(flying, parts):
        for c in group:
            c.wait_recv()
        at = box(xg, "oir", start, rows, core)
        across.append(wire.copy(xg.at[at], xg.at[at], sibling))

    def forward(core_at):
        acc = None
        for o in range(n_o):
            for i in range(n_i):
                s = (o * n_i + i) * 2 + core_at
                d = jnp.dot(a_v[s], xg[o, i, core_at].reshape(slab, width), preferred_element_type=F32)
                acc = d if acc is None else acc + d
        return acc

    aggp[...] = forward(core)
    for c in across:
        c.wait_recv()
    aggp[...] = aggp[...] + forward(sib)

    aggs[...] = aggp[...].astype(BF).reshape(n_r, share, width)
    flying = [wire.copy(aggs.at[to], aggr.at[k - 1], d) for k, to, d in peers("r")]
    agg_sum = aggp[pl.ds(mine, share), :]
    for c in flying:
        c.wait_recv()
    for k in range(1, n_r):
        agg_sum = agg_sum + aggr[k - 1].astype(F32)
    degm = degc[pl.ds(mine, share), :]
    deg = jnp.concatenate([degm] * (width // 128), axis=1)
    agg = (agg_sum / deg).astype(BF)
    pre = xw[...] + jnp.dot(agg, wn_ref[...], preferred_element_type=F32) + bias_ref[...].reshape(1, width)
    sig = jax.nn.sigmoid(pre)
    hid_ref[...] = (pre * sig).astype(BF)
    cot = cot_ref[pl.ds(mine, share), :].astype(F32)
    dpre = (cot * (sig * (1.0 + pre * (1.0 - sig)))).astype(BF)
    dagg = lax.dot_general(dpre, wn_ref[...], NT, preferred_element_type=F32) / deg
    dg[rep] = dagg.astype(BF)
    flying = [wire.copy(dg.at[rep], dg.at[rep], d) for _, _, d in peers("r")]

    piece = g_v.shape[1:-1]
    g_v[0] = jnp.dot(xt[...], dpre, preferred_element_type=F32).astype(BF).reshape(piece + (width,))
    g_v[1] = jnp.dot(agg.T, dpre, preferred_element_type=F32).astype(BF).reshape(piece + (width,))
    grads = [wire.copy(g_v.at[sib], g_core, sibling)]
    bias_sum = jnp.sum(dpre.astype(F32), axis=0, keepdims=True)
    b_core[core] = jnp.broadcast_to(bias_sum, (8, width))
    biases = [wire.copy(b_core.at[core], b_core.at[core], sibling)]
    selfp[...] = lax.dot_general(dpre, ws_ref[...], NT, preferred_element_type=F32)

    for c in flying:
        c.wait_recv()
    dgs = dg[...].reshape(slab, width)

    def backward(o, i, core_at):
        s = (o * n_i + i) * 2 + core_at
        return jnp.dot(at_v[s], dgs, preferred_element_type=F32)

    across = []
    for o in range(n_o):
        for i in range(n_i):
            part_v[o, i, sib] = backward(o, i, sib).astype(BF).reshape(n_r, share, width)
        across.append(wire.copy(part_v.at[o, :, sib], core_in.at[o], sibling))

    def bias_stage(b_ref, at, axis):
        b_ref[at] = bias_total[0]
        return [wire.copy(b_ref.at[at], b_ref.at[at], d) for _, _, d in peers(axis)]

    bias_total = [None]

    def bias_add(copies, b_ref, n):
        for c in copies:
            c.wait_recv()
        total = b_ref[0]
        for k in range(1, n):
            total = total + b_ref[k]
        bias_total[0] = total

    bias_add(biases, b_core, 2)
    grads[0].wait_recv()
    g_v[core] = (g_v[core].astype(F32) + g_core[...].astype(F32)).astype(BF)
    grads = [wire.copy(g_v.at[core, to], g_in.at[k - 1], d) for k, to, d in peers("i")]
    biases = bias_stage(b_in, me["i"], "i")

    for o in range(n_o):
        across[o].wait_recv()
        for i in range(n_i):
            total = backward(o, i, core) + core_in[o, i].astype(F32).reshape(slab, width)
            part_v[o, i, core] = total.astype(BF).reshape(n_r, share, width)

    def scatter_stage(n):
        sent = []
        for p, (start, rows, order) in enumerate(parts):
            axis = order[2 - n]
            sent.append([
                wire.copy(
                    part_v.at[box(part_v, order[:2 - n], start, rows, core, (axis, to))],
                    slots[3 * p + n].at[k - 1], d,
                )
                for k, to, d in peers(axis)
            ])
        return sent

    def scatter_add(n, sent):
        for p, (start, rows, order) in enumerate(parts):
            at = box(part_v, order[:2 - n], start, rows, core)
            total = part_v[at].astype(F32)
            for k, c in enumerate(sent[p]):
                c.wait_recv()
                total = total + slots[3 * p + n][k].astype(F32)
            if n < 2:
                part_v[at] = total.astype(BF)
            else:
                fg_ref[start:start + rows, :] = (selfp[start:start + rows, :] + total).astype(BF)

    sent = scatter_stage(0)

    for c in grads:
        c.wait_recv()
    total = g_v[core, me["i"]].astype(F32)
    for k in range(1, n_i):
        total = total + g_in[k - 1].astype(F32)
    g_v[core, me["i"]] = total.astype(BF)
    grads = [wire.copy(g_v.at[core, me["i"], to], g_out.at[k - 1], d) for k, to, d in peers("o")]
    bias_add(biases, b_in, n_i)
    biases = bias_stage(b_out, me["o"], "o")

    scatter_add(0, sent)
    sent = scatter_stage(1)

    for c in grads:
        c.wait_recv()
    total = g_v[core, me["i"], me["o"]].astype(F32)
    for k in range(1, n_o):
        total = total + g_out[k - 1].astype(F32)
    g_rep[rep] = total.astype(BF)
    grads = [wire.copy(g_rep.at[rep], g_rep.at[rep], d) for _, _, d in peers("r")]
    bias_add(biases, b_out, n_o)
    biases = bias_stage(b_rep, rep, "r")

    scatter_add(1, sent)
    sent = scatter_stage(2)

    for c in grads:
        c.wait_recv()
    total = g_rep[0].astype(F32)
    for k in range(1, n_r):
        total = total + g_rep[k].astype(F32)
    at = (core, me["i"], me["o"])
    ga[at] = total.astype(BF)
    grads = [wire.copy(ga.at[at], ga.at[at], d) for _, _, d in peers("o")]
    bias_add(biases, b_rep, n_r)
    gb_ref[...] = bias_total[0][0:1, :].reshape(width)

    for c in grads:
        c.wait_recv()
    at = (core, me["i"])
    grads = [wire.copy(ga.at[at], ga.at[at], d) for _, _, d in peers("i")]

    scatter_add(2, sent)

    for c in grads:
        c.wait_recv()
    last = wire.copy(ga.at[core], ga.at[core], sibling)
    last.wait_recv()
    gs_ref[...] = ga[0].astype(F32).reshape(width, width)
    gn_ref[...] = ga[1].astype(F32).reshape(width, width)

    for c in wire.copies:
        c.wait_send()


def shards(n_blk, n_rep, features, degree, tiles, block_rows, block_cols, live, w_self, w_neigh, bias, cotangent):
    _, _, nslab, cap, tile, _ = tiles.shape
    slab, width = features.shape
    share = slab // n_rep
    n_i = 2
    n_o = n_blk // (2 * n_i)
    sizes = {"o": n_o, "i": n_i, "r": n_rep}
    parts = split_rows(share)
    grows = width // (n_i * n_o)
    nodes = (n_o, n_i, 2, n_rep, share, width)
    ncopy = 8 + (len(parts) + 1) * 2 * (n_o + n_i + n_rep) + n_o * 3 + n_i * 3 + n_rep * 4
    vmem = pl.BlockSpec(memory_space=pltpu.VMEM)
    smem = pl.BlockSpec(memory_space=pltpu.SMEM)
    scratch = [
        pltpu.VMEM((nslab, cap, tile, tile), BF),
        pltpu.VMEM((nslab, slab, slab), BF),
        pltpu.VMEM((nslab, slab, slab), BF),
        pltpu.VMEM(nodes, BF),
        pltpu.VMEM(nodes, BF),
        pltpu.VMEM((share, width), F32),
        pltpu.VMEM((slab, 128), F32),
        pltpu.VMEM((width, share), BF),
        pltpu.VMEM((slab, width), F32),
        pltpu.VMEM((n_rep, share, width), BF),
        pltpu.VMEM((max(1, n_rep - 1), share, width), BF),
        pltpu.VMEM((n_rep, share, width), BF),
        pltpu.VMEM((n_o, n_i, n_rep, share, width), BF),
        pltpu.VMEM((share, width), F32),
        pltpu.VMEM((2, n_i, n_o, grows, width), BF),
        pltpu.VMEM((n_i, n_o, grows, width), BF),
        pltpu.VMEM((n_i - 1, n_o, grows, width), BF),
        pltpu.VMEM((n_o - 1, grows, width), BF),
        pltpu.VMEM((n_rep, grows, width), BF),
        pltpu.VMEM((2, n_i, n_o, grows, width), BF),
        pltpu.VMEM((2, 8, width), F32),
        pltpu.VMEM((n_i, 8, width), F32),
        pltpu.VMEM((n_o, 8, width), F32),
        pltpu.VMEM((n_rep, 8, width), F32),
        pltpu.SemaphoreType.DMA((ncopy,)),
        pltpu.SemaphoreType.DMA((ncopy,)),
        pltpu.SemaphoreType.DMA,
    ] + [pltpu.VMEM(s, BF) for s in slot_shapes(parts, sizes, width)]
    return pl.pallas_call(
        functools.partial(kernel, sizes, parts, nslab, cap, tile, width, slab, share),
        out_shape=(
            jax.ShapeDtypeStruct((share, width), BF),
            jax.ShapeDtypeStruct((share, width), BF),
            jax.ShapeDtypeStruct((width, width), F32),
            jax.ShapeDtypeStruct((width, width), F32),
            jax.ShapeDtypeStruct((width,), F32),
        ),
        in_specs=[vmem, vmem, pl.BlockSpec(memory_space=pl.ANY), smem, smem, smem, vmem, vmem, vmem, vmem],
        out_specs=(vmem,) * 5,
        scratch_shapes=scratch,
        compiler_params=pltpu.CompilerParams(
            collective_id=0, has_side_effects=True, vmem_limit_bytes=56 * 1024 * 1024
        ),
        cost_estimate=pl.CostEstimate(
            flops=4 * slab * nslab * slab * width, bytes_accessed=2 * tiles.size, transcendentals=share * width
        ),
        name="sage_layer",
    )(features, degree, tiles, block_rows, block_cols, live, w_self, w_neigh, bias, cotangent)


def solution(mesh):
    n_blk, n_rep = mesh.shape["blk"], mesh.shape["rep"]
    return jax.shard_map(
        functools.partial(shards, n_blk, n_rep),
        mesh=mesh,
        in_specs=(
            P("blk", None),
            P("blk"),
            P("blk", "rep", None, None, None, None),
            P("blk", "rep", None, None),
            P("blk", "rep", None, None),
            P("blk", "rep", None),
            P(),
            P(),
            P(),
            P("blk", None),
        ),
        out_specs=(P(("blk", "rep"), None), P(("blk", "rep"), None), P(), P(), P()),
        check_vma=False,
    )
```

```python
import functools

import jax
import jax.numpy as jnp
from jax import lax
from jax.experimental import pallas as pl
from jax.experimental.pallas import tpu as pltpu
from jax.sharding import PartitionSpec as P

BF = jnp.bfloat16
F32 = jnp.float32
MESH = pl.DeviceIdType.MESH
NT = (((1,), (1,)), ((), ()))
ROWS = 16
STRIP = 32


def split_rows(share):
    units = share // ROWS
    side = max(1, units * 3 // 8)
    sizes = [side, units - 2 * side, side]
    orders = ["oir", "iro", "roi"]
    parts, at = [], 0
    for size, order in zip(sizes, orders):
        if size > 0:
            parts.append((at * ROWS, size * ROWS, order))
            at += size
    return parts


def slot_shapes(parts, sizes, width):
    shapes = []
    for _, rows, order in parts:
        left = dict(sizes)
        for axis in reversed(order):
            peers = left.pop(axis) - 1
            shapes.append((peers,) + tuple(left[a] for a in "oir" if a in left) + (rows, width))
    return shapes


class Wire:
    def __init__(self, send, recv):
        self.send, self.recv, self.copies = send, recv, []

    def copy(self, src, dst, device):
        k = len(self.copies)
        c = pltpu.make_async_remote_copy(
            src_ref=src, dst_ref=dst, send_sem=self.send.at[k], recv_sem=self.recv.at[k],
            device_id=device, device_id_type=MESH,
        )
        c.start()
        self.copies.append(c)
        return c


def kernel(
    sizes, parts, nslab, cap, tile, width, slab, share,
    x_ref, deg_ref, tiles_ref, rows_ref, cols_ref, live_ref, ws_hbm, wn_hbm, bias_ref, cot_hbm,
    hid_ref, fg_ref, ga, gb_ref,
    tv, a_v, at_v, xg, part_v, xw, degc, xt, aggp, aggs, aggr, dg, core_in, selfp,
    g_v, g_core, g_chip, g_rep, b_core, b_chip, b_rep, ws_v, wn_v, cot_v,
    send_sem, recv_sem, local_sem, *slots,
):
    n_o, n_i, n_r = sizes["o"], sizes["i"], sizes["r"]
    nb = slab // tile
    blk = lax.axis_index("blk")
    rep = lax.axis_index("rep")
    core = lax.rem(blk, 2)
    sib = 1 - core
    me = {"o": blk // (2 * n_i), "i": lax.rem(blk // 2, n_i), "r": rep}
    wire = Wire(send_sem, recv_sem)

    def device(axis, to):
        at = dict(me)
        at[axis] = to
        return ((at["o"] * n_i + at["i"]) * 2 + core, at["r"])

    sibling = ((me["o"] * n_i + me["i"]) * 2 + sib, rep)

    def peers(axis):
        for k in range(1, sizes[axis]):
            to = lax.rem(me[axis] + k, sizes[axis])
            yield k, to, device(axis, to)

    n_c = n_o * n_i
    chip = blk // 2

    def chips():
        for k in range(1, n_c):
            to = lax.rem(chip + k, n_c)
            yield k, to, (to * 2 + core, rep)

    loads = [
        pltpu.make_async_copy(src, dst, local_sem.at[k])
        for k, (src, dst) in enumerate(
            [(tiles_ref.at[0, 0], tv), (ws_hbm, ws_v), (wn_hbm, wn_v), (cot_hbm, cot_v)]
        )
    ]
    for c in loads:
        c.start()

    mine = pl.multiple_of(rep * share, share)
    x_mine = x_ref[pl.ds(mine, share), :]
    xg[me["o"], me["i"], core, rep] = x_mine
    for start, rows, order in parts:
        if order[0] == "r":
            for k in range(n_r):
                at = k * share + start
                xg[me["o"], me["i"], core, k, start:start + rows, :] = x_ref[at:at + rows, :]

    barrier = pltpu.get_barrier_semaphore()
    everyone = [sibling] + [d for _, _, d in chips()] + [d for _, _, d in peers("r")]
    for d in everyone:
        pl.semaphore_signal(barrier, inc=1, device_id=d, device_id_type=MESH)
    pl.semaphore_wait(barrier, len(everyone))

    def box(ref, have, start, rows, core_at, fixed=None):
        at = [slice(None) if a in have else me[a] for a in "oir"]
        if fixed is not None:
            at["oir".index(fixed[0])] = fixed[1]
        return (at[0], at[1], core_at, at[2], pl.ds(start, rows), slice(None))

    def gather(p, n):
        start, rows, order = parts[p]
        if n == 0 and order[0] == "r":
            return []
        if n == 3:
            at = box(xg, "oir", start, rows, core)
            return [wire.copy(xg.at[at], xg.at[at], sibling)]
        at = box(xg, order[:n], start, rows, core)
        return [wire.copy(xg.at[at], xg.at[at], d) for _, _, d in peers(order[n])]

    def arrived(copies):
        for c in copies:
            c.wait_recv()

    every = range(len(parts))
    lead = [p for p in every if parts[p][2][0] == "r"]
    rest = [p for p in every if p not in lead]

    flying = {p: gather(p, 0) for p in rest}
    for p in lead:
        flying[p] = gather(p, 1)

    loads[0].wait()

    def build(s, carry):
        live = live_ref[0, 0, s]
        weights = []
        for c in range(cap):
            row, col = rows_ref[0, 0, c, s], cols_ref[0, 0, c, s]
            used = c < live
            weights.append([
                [jnp.where(used & (row == i) & (col == j), 1.0, 0.0).astype(F32) for j in range(nb)]
                for i in range(nb)
            ])
        for r0 in range(0, tile, STRIP):
            acc = [[jnp.zeros((STRIP, tile), F32) for _ in range(nb)] for _ in range(nb)]
            for c in range(cap):
                t = tv[s, c, r0:r0 + STRIP, :].astype(F32)
                for i in range(nb):
                    for j in range(nb):
                        acc[i][j] = acc[i][j] + t * weights[c][i][j]
            for i in range(nb):
                for j in range(nb):
                    a_v[s, i * tile + r0:i * tile + r0 + STRIP, j * tile:(j + 1) * tile] = acc[i][j].astype(BF)
        at_v[s] = a_v[s].T
        return carry

    half = nslab // 2
    lax.fori_loop(0, half, build, 0)

    for p in reversed(rest):
        arrived(flying[p])
        flying[p] = gather(p, 1)

    lax.fori_loop(half, nslab, build, 0)
    for c in loads[1:]:
        c.wait()
    xw[...] = jnp.dot(x_mine, ws_v[...], preferred_element_type=F32)
    xt[...] = x_mine.T
    degf = deg_ref[...].astype(F32).reshape(1, slab)
    degc[...] = jnp.broadcast_to(degf, (128, slab)).T

    for p in list(reversed(rest)) + lead:
        arrived(flying[p])
        flying[p] = gather(p, 2)
    for p in rest[:1] + lead + rest[1:]:
        arrived(flying[p])
        flying[p] = gather(p, 3)

    def forward(core_at):
        acc = None
        for o in range(n_o):
            for i in range(n_i):
                s = (o * n_i + i) * 2 + core_at
                d = jnp.dot(a_v[s], xg[o, i, core_at].reshape(slab, width), preferred_element_type=F32)
                acc = d if acc is None else acc + d
        return acc

    aggp[...] = forward(core)
    for p in every:
        arrived(flying[p])
    aggp[...] = aggp[...] + forward(sib)

    aggs[...] = aggp[...].astype(BF).reshape(n_r, share, width)
    flying = [wire.copy(aggs.at[to], aggr.at[k - 1], d) for k, to, d in peers("r")]
    agg_sum = aggp[pl.ds(mine, share), :]
    for c in flying:
        c.wait_recv()
    for k in range(1, n_r):
        agg_sum = agg_sum + aggr[k - 1].astype(F32)
    degm = degc[pl.ds(mine, share), :]
    deg = jnp.concatenate([degm] * (width // 128), axis=1)
    agg = (agg_sum / deg).astype(BF)
    pre = xw[...] + jnp.dot(agg, wn_v[...], preferred_element_type=F32) + bias_ref[...].reshape(1, width)
    sig = jax.nn.sigmoid(pre)
    hid_ref[...] = (pre * sig).astype(BF)
    cot = cot_v[pl.ds(mine, share), :].astype(F32)
    dpre = (cot * (sig * (1.0 + pre * (1.0 - sig)))).astype(BF)
    dagg = lax.dot_general(dpre, wn_v[...], NT, preferred_element_type=F32) / deg
    dg[rep] = dagg.astype(BF)
    flying = [wire.copy(dg.at[rep], dg.at[rep], d) for _, _, d in peers("r")]

    piece = g_v.shape[1:-1]
    g_v[0] = jnp.dot(xt[...], dpre, preferred_element_type=F32).astype(BF).reshape(piece + (width,))
    g_v[1] = jnp.dot(agg.T, dpre, preferred_element_type=F32).astype(BF).reshape(piece + (width,))
    grads = [wire.copy(g_v.at[sib], g_core, sibling)]
    bias_sum = jnp.sum(dpre.astype(F32), axis=0, keepdims=True)
    b_core[core] = jnp.broadcast_to(bias_sum, (8, width))
    biases = [wire.copy(b_core.at[core], b_core.at[core], sibling)]
    selfp[...] = lax.dot_general(dpre, ws_v[...], NT, preferred_element_type=F32)

    for c in flying:
        c.wait_recv()
    dgs = dg[...].reshape(slab, width)

    def backward(o, i, core_at):
        s = (o * n_i + i) * 2 + core_at
        return jnp.dot(at_v[s], dgs, preferred_element_type=F32)

    across = []
    for o in range(n_o):
        for i in range(n_i):
            part_v[o, i, sib] = backward(o, i, sib).astype(BF).reshape(n_r, share, width)
        across.append(wire.copy(part_v.at[o, :, sib], core_in.at[o], sibling))

    def bias_sum_of(b_ref, n):
        total = b_ref[0]
        for k in range(1, n):
            total = total + b_ref[k]
        return total

    arrived(grads + biases)
    g_v[core] = (g_v[core].astype(F32) + g_core[...].astype(F32)).astype(BF)
    grads = [wire.copy(g_v.at[core, to], g_chip.at[k - 1], d) for k, to, d in chips()]
    b_chip[chip] = bias_sum_of(b_core, 2)
    biases = [wire.copy(b_chip.at[chip], b_chip.at[chip], d) for _, _, d in chips()]

    for o in range(n_o):
        across[o].wait_recv()
        for i in range(n_i):
            total = backward(o, i, core) + core_in[o, i].astype(F32).reshape(slab, width)
            part_v[o, i, core] = total.astype(BF).reshape(n_r, share, width)

    def scatter(p, n):
        start, rows, order = parts[p]
        axis = order[2 - n]
        return [
            wire.copy(
                part_v.at[box(part_v, order[:2 - n], start, rows, core, (axis, to))],
                slots[3 * p + n].at[k - 1], d,
            )
            for k, to, d in peers(axis)
        ]

    def scatter_add(p, n, sent):
        start, rows, order = parts[p]
        at = box(part_v, order[:2 - n], start, rows, core)
        arrived(sent)
        total = part_v[at].astype(F32)
        for k in range(len(sent)):
            total = total + slots[3 * p + n][k].astype(F32)
        if n < 2:
            part_v[at] = total.astype(BF)
        else:
            fg_ref[start:start + rows, :] = (selfp[start:start + rows, :] + total).astype(BF)

    turns = rest[:1] + lead + rest[1:]
    sent = {p: scatter(p, 0) for p in every}

    arrived(grads + biases)
    total = g_v[core, chip].astype(F32)
    for k in range(1, n_c):
        total = total + g_chip[k - 1].astype(F32)
    g_rep[rep] = total.astype(BF)
    grads = [wire.copy(g_rep.at[rep], g_rep.at[rep], d) for _, _, d in peers("r")]
    b_rep[rep] = bias_sum_of(b_chip, n_c)
    biases = [wire.copy(b_rep.at[rep], b_rep.at[rep], d) for _, _, d in peers("r")]

    for p in turns:
        scatter_add(p, 0, sent[p])
        sent[p] = scatter(p, 1)

    arrived(grads + biases)
    total = g_rep[0].astype(F32)
    for k in range(1, n_r):
        total = total + g_rep[k].astype(F32)
    ga[core, chip] = total.astype(BF)
    grads = [wire.copy(ga.at[core, chip], ga.at[core, chip], d) for _, _, d in chips()]
    gb_ref[...] = bias_sum_of(b_rep, n_r)

    for p in turns:
        scatter_add(p, 1, sent[p])
        sent[p] = scatter(p, 2)

    arrived(grads)
    last = wire.copy(ga.at[core], ga.at[core], sibling)
    for p in turns:
        scatter_add(p, 2, sent[p])
    last.wait_recv()

    for c in wire.copies:
        c.wait_send()


def finish(hid_in, fg_in, ga, gb_in, hid_ref, fg_ref, gs_ref, gn_ref, gb_ref):
    width = gs_ref.shape[0]
    hid_ref[...] = hid_in[...]
    fg_ref[...] = fg_in[...]
    gs_ref[...] = ga[0].astype(F32).reshape(width, width)
    gn_ref[...] = ga[1].astype(F32).reshape(width, width)
    gb_ref[...] = gb_in[0:1, :].reshape(width)


def shards(n_blk, n_rep, features, degree, tiles, block_rows, block_cols, live, w_self, w_neigh, bias, cotangent):
    _, _, nslab, cap, tile, _ = tiles.shape
    slab, width = features.shape
    share = slab // n_rep
    n_i = 2
    n_o = n_blk // (2 * n_i)
    sizes = {"o": n_o, "i": n_i, "r": n_rep}
    parts = split_rows(share)
    n_c = n_o * n_i
    grows = width // n_c
    nodes = (n_o, n_i, 2, n_rep, share, width)
    ncopy = 8 + (len(parts) + 1) * 2 * (n_o + n_i + n_rep) + n_o + n_c * 3 + n_rep * 4
    vmem = pl.BlockSpec(memory_space=pltpu.VMEM)
    smem = pl.BlockSpec(memory_space=pltpu.SMEM)
    scratch = [
        pltpu.VMEM((nslab, cap, tile, tile), BF),
        pltpu.VMEM((nslab, slab, slab), BF),
        pltpu.VMEM((nslab, slab, slab), BF),
        pltpu.VMEM(nodes, BF),
        pltpu.VMEM(nodes, BF),
        pltpu.VMEM((share, width), F32),
        pltpu.VMEM((slab, 128), F32),
        pltpu.VMEM((width, share), BF),
        pltpu.VMEM((slab, width), F32),
        pltpu.VMEM((n_rep, share, width), BF),
        pltpu.VMEM((max(1, n_rep - 1), share, width), BF),
        pltpu.VMEM((n_rep, share, width), BF),
        pltpu.VMEM((n_o, n_i, n_rep, share, width), BF),
        pltpu.VMEM((share, width), F32),
        pltpu.VMEM((2, n_c, grows, width), BF),
        pltpu.VMEM((n_c, grows, width), BF),
        pltpu.VMEM((n_c - 1, grows, width), BF),
        pltpu.VMEM((n_rep, grows, width), BF),
        pltpu.VMEM((2, 8, width), F32),
        pltpu.VMEM((n_c, 8, width), F32),
        pltpu.VMEM((n_rep, 8, width), F32),
        pltpu.VMEM((width, width), BF),
        pltpu.VMEM((width, width), BF),
        pltpu.VMEM((slab, width), BF),
        pltpu.SemaphoreType.DMA((ncopy,)),
        pltpu.SemaphoreType.DMA((ncopy,)),
        pltpu.SemaphoreType.DMA((4,)),
    ] + [pltpu.VMEM(s, BF) for s in slot_shapes(parts, sizes, width)]
    anywhere = pl.BlockSpec(memory_space=pl.ANY)
    done = pl.pallas_call(
        functools.partial(kernel, sizes, parts, nslab, cap, tile, width, slab, share),
        out_shape=(
            jax.ShapeDtypeStruct((share, width), BF),
            jax.ShapeDtypeStruct((share, width), BF),
            jax.ShapeDtypeStruct((2, n_c, grows, width), BF),
            jax.ShapeDtypeStruct((8, width), F32),
        ),
        in_specs=[vmem, vmem, anywhere, smem, smem, smem, anywhere, anywhere, vmem, anywhere],
        out_specs=(vmem,) * 4,
        scratch_shapes=scratch,
        compiler_params=pltpu.CompilerParams(
            collective_id=0, has_side_effects=True, vmem_limit_bytes=56 * 1024 * 1024
        ),
        cost_estimate=pl.CostEstimate(
            flops=4 * slab * nslab * slab * width, bytes_accessed=2 * tiles.size, transcendentals=share * width
        ),
        name="sage_layer",
    )(features, degree, tiles, jnp.swapaxes(block_rows, 2, 3), jnp.swapaxes(block_cols, 2, 3), live, w_self, w_neigh, bias, cotangent)
    return pl.pallas_call(
        finish,
        out_shape=(
            jax.ShapeDtypeStruct((share, width), BF),
            jax.ShapeDtypeStruct((share, width), BF),
            jax.ShapeDtypeStruct((width, width), F32),
            jax.ShapeDtypeStruct((width, width), F32),
            jax.ShapeDtypeStruct((width,), F32),
        ),
        in_specs=[vmem] * 4,
        out_specs=(vmem,) * 5,
        name="write_results",
    )(*done)


def solution(mesh):
    n_blk, n_rep = mesh.shape["blk"], mesh.shape["rep"]
    return jax.shard_map(
        functools.partial(shards, n_blk, n_rep),
        mesh=mesh,
        in_specs=(
            P("blk", None),
            P("blk"),
            P("blk", "rep", None, None, None, None),
            P("blk", "rep", None, None),
            P("blk", "rep", None, None),
            P("blk", "rep", None),
            P(),
            P(),
            P(),
            P("blk", None),
        ),
        out_specs=(P(("blk", "rep"), None), P(("blk", "rep"), None), P(), P(), P()),
        check_vma=False,
    )
```

```python
import functools

import jax
import jax.numpy as jnp
from jax import lax
from jax.experimental import pallas as pl
from jax.experimental.pallas import tpu as pltpu
from jax.sharding import PartitionSpec as P

BF = jnp.bfloat16
F32 = jnp.float32
MESH = pl.DeviceIdType.MESH
NT = (((1,), (1,)), ((), ()))
ROWS = 16
STRIP = 32


def split_rows(share):
    units = share // ROWS
    side = max(1, units * 3 // 8)
    sizes = [side, units - 2 * side, side]
    orders = ["oir", "iro", "roi"]
    parts, at = [], 0
    for size, order in zip(sizes, orders):
        if size > 0:
            parts.append((at * ROWS, size * ROWS, order))
            at += size
    return parts


def slot_shapes(parts, sizes, width):
    shapes = []
    for _, rows, order in parts:
        left = dict(sizes)
        for axis in reversed(order):
            peers = left.pop(axis) - 1
            shapes.append((peers,) + tuple(left[a] for a in "oir" if a in left) + (rows, width))
    return shapes


class Wire:
    def __init__(self, send, recv):
        self.send, self.recv, self.copies = send, recv, []

    def copy(self, src, dst, device):
        k = len(self.copies)
        c = pltpu.make_async_remote_copy(
            src_ref=src, dst_ref=dst, send_sem=self.send.at[k], recv_sem=self.recv.at[k],
            device_id=device, device_id_type=MESH,
        )
        c.start()
        self.copies.append(c)
        return c


def kernel(
    sizes, parts, nslab, cap, tile, width, slab, share,
    x_ref, deg_ref, tiles_ref, rows_ref, cols_ref, live_ref, ws_hbm, wn_hbm, bias_ref, cot_hbm,
    hid_ref, fg_ref, ga, gb_ref,
    tv, a_v, at_v, xg, part_v, xw, degc, xt, aggp, aggs, aggr, dg, core_in, selfp,
    g_v, g_core, g_chip, g_rep, b_core, b_chip, b_rep, ws_v, wn_v, cot_v,
    send_sem, recv_sem, local_sem, *slots,
):
    n_o, n_i, n_r = sizes["o"], sizes["i"], sizes["r"]
    nb = slab // tile
    blk = lax.axis_index("blk")
    rep = lax.axis_index("rep")
    core = lax.rem(blk, 2)
    sib = 1 - core
    me = {"o": blk // (2 * n_i), "i": lax.rem(blk // 2, n_i), "r": rep}
    wire = Wire(send_sem, recv_sem)

    def device(axis, to):
        at = dict(me)
        at[axis] = to
        return ((at["o"] * n_i + at["i"]) * 2 + core, at["r"])

    sibling = ((me["o"] * n_i + me["i"]) * 2 + sib, rep)

    def peers(axis):
        for k in range(1, sizes[axis]):
            to = lax.rem(me[axis] + k, sizes[axis])
            yield k, to, device(axis, to)

    n_c = n_o * n_i
    chip = blk // 2

    def chips():
        for k in range(1, n_c):
            to = lax.rem(chip + k, n_c)
            yield k, to, (to * 2 + core, rep)

    loads = [
        pltpu.make_async_copy(src, dst, local_sem.at[k])
        for k, (src, dst) in enumerate(
            [(tiles_ref.at[0, 0], tv), (ws_hbm, ws_v), (wn_hbm, wn_v), (cot_hbm, cot_v)]
        )
    ]
    for c in loads:
        c.start()

    mine = pl.multiple_of(rep * share, share)
    x_mine = x_ref[pl.ds(mine, share), :]
    xg[me["o"], me["i"], core, rep] = x_mine
    for start, rows, order in parts:
        if order[0] == "r":
            for k in range(n_r):
                at = k * share + start
                xg[me["o"], me["i"], core, k, start:start + rows, :] = x_ref[at:at + rows, :]

    barrier = pltpu.get_barrier_semaphore()
    everyone = [sibling] + [d for _, _, d in chips()] + [d for _, _, d in peers("r")]
    for d in everyone:
        pl.semaphore_signal(barrier, inc=1, device_id=d, device_id_type=MESH)
    pl.semaphore_wait(barrier, len(everyone))

    def box(ref, have, start, rows, core_at, fixed=None):
        at = [slice(None) if a in have else me[a] for a in "oir"]
        if fixed is not None:
            at["oir".index(fixed[0])] = fixed[1]
        return (at[0], at[1], core_at, at[2], pl.ds(start, rows), slice(None))

    def gather(p, n):
        start, rows, order = parts[p]
        if n == 0 and order[0] == "r":
            return []
        if n == 3:
            at = box(xg, "oir", start, rows, core)
            return [wire.copy(xg.at[at], xg.at[at], sibling)]
        at = box(xg, order[:n], start, rows, core)
        return [wire.copy(xg.at[at], xg.at[at], d) for _, _, d in peers(order[n])]

    def arrived(copies):
        for c in copies:
            c.wait_recv()

    every = range(len(parts))
    lead = [p for p in every if parts[p][2][0] == "r"]
    rest = [p for p in every if p not in lead]

    flying = {p: gather(p, 0) for p in rest}
    for p in lead:
        flying[p] = gather(p, 1)

    loads[0].wait()

    def build(s, carry):
        live = live_ref[0, 0, s]
        weights = []
        for c in range(cap):
            row, col = rows_ref[0, 0, c, s], cols_ref[0, 0, c, s]
            used = c < live
            weights.append([
                [jnp.where(used & (row == i) & (col == j), 1.0, 0.0).astype(F32) for j in range(nb)]
                for i in range(nb)
            ])
        for r0 in range(0, tile, STRIP):
            acc = [[jnp.zeros((STRIP, tile), F32) for _ in range(nb)] for _ in range(nb)]
            for c in range(cap):
                t = tv[s, c, r0:r0 + STRIP, :].astype(F32)
                for i in range(nb):
                    for j in range(nb):
                        acc[i][j] = acc[i][j] + t * weights[c][i][j]
            for i in range(nb):
                for j in range(nb):
                    a_v[s, i * tile + r0:i * tile + r0 + STRIP, j * tile:(j + 1) * tile] = acc[i][j].astype(BF)
        at_v[s] = a_v[s].T
        return carry

    half = nslab // 2
    lax.fori_loop(0, half, build, 0)

    for p in reversed(rest):
        arrived(flying[p])
        flying[p] = gather(p, 1)

    lax.fori_loop(half, nslab, build, 0)
    for c in loads[1:]:
        c.wait()
    xw[...] = jnp.dot(x_mine, ws_v[...], preferred_element_type=F32)
    xt[...] = x_mine.T
    degf = deg_ref[...].astype(F32).reshape(1, slab)
    degc[...] = jnp.broadcast_to(degf, (128, slab)).T

    for p in list(reversed(rest)) + lead:
        arrived(flying[p])
        flying[p] = gather(p, 2)
    for p in rest[:1] + lead + rest[1:]:
        arrived(flying[p])
        flying[p] = gather(p, 3)

    def forward(core_at):
        acc = None
        for o in range(n_o):
            for i in range(n_i):
                s = (o * n_i + i) * 2 + core_at
                d = jnp.dot(a_v[s], xg[o, i, core_at].reshape(slab, width), preferred_element_type=F32)
                acc = d if acc is None else acc + d
        return acc

    aggp[...] = forward(core)
    for p in every:
        arrived(flying[p])
    aggp[...] = aggp[...] + forward(sib)

    aggs[...] = aggp[...].astype(BF).reshape(n_r, share, width)
    flying = [wire.copy(aggs.at[to], aggr.at[k - 1], d) for k, to, d in peers("r")]
    agg_sum = aggp[pl.ds(mine, share), :]
    for c in flying:
        c.wait_recv()
    for k in range(1, n_r):
        agg_sum = agg_sum + aggr[k - 1].astype(F32)
    degm = degc[pl.ds(mine, share), :]
    deg = jnp.concatenate([degm] * (width // 128), axis=1)
    agg = (agg_sum / deg).astype(BF)
    pre = xw[...] + jnp.dot(agg, wn_v[...], preferred_element_type=F32) + bias_ref[...].reshape(1, width)
    sig = jax.nn.sigmoid(pre)
    cot = cot_v[pl.ds(mine, share), :].astype(F32)
    dpre = (cot * (sig * (1.0 + pre * (1.0 - sig)))).astype(BF)
    dagg = lax.dot_general(dpre, wn_v[...], NT, preferred_element_type=F32) / deg
    dg[rep] = dagg.astype(BF)
    flying = [wire.copy(dg.at[rep], dg.at[rep], d) for _, _, d in peers("r")]

    hid_ref[...] = (pre * sig).astype(BF)
    piece = g_v.shape[1:-1]
    g_v[0] = jnp.dot(xt[...], dpre, preferred_element_type=F32).astype(BF).reshape(piece + (width,))
    g_v[1] = jnp.dot(agg.T, dpre, preferred_element_type=F32).astype(BF).reshape(piece + (width,))
    grads = [wire.copy(g_v.at[sib], g_core, sibling)]
    bias_sum = jnp.sum(dpre.astype(F32), axis=0, keepdims=True)
    b_core[core] = bias_sum
    biases = [wire.copy(b_core.at[core], b_core.at[core], sibling)]
    selfp[...] = lax.dot_general(dpre, ws_v[...], NT, preferred_element_type=F32)

    for c in flying:
        c.wait_recv()
    dgs = dg[...].reshape(slab, width)

    def backward(o, i, core_at):
        s = (o * n_i + i) * 2 + core_at
        return jnp.dot(at_v[s], dgs, preferred_element_type=F32)

    def bias_sum_of(b_ref, n):
        total = b_ref[0]
        for k in range(1, n):
            total = total + b_ref[k]
        return total

    arrived(grads + biases)
    g_v[core] = (g_v[core].astype(F32) + g_core[...].astype(F32)).astype(BF)
    grads = [wire.copy(g_v.at[core, to], g_chip.at[k - 1], d) for k, to, d in chips()]
    b_chip[chip] = bias_sum_of(b_core, 2)
    biases = [wire.copy(b_chip.at[chip], b_chip.at[chip], d) for _, _, d in chips()]

    across = []
    for o in range(n_o):
        for i in range(n_i):
            part_v[o, i, sib] = backward(o, i, sib).astype(BF).reshape(n_r, share, width)
        across.append(wire.copy(part_v.at[o, :, sib], core_in.at[o], sibling))

    for o in range(n_o):
        across[o].wait_recv()
        for i in range(n_i):
            total = backward(o, i, core) + core_in[o, i].astype(F32).reshape(slab, width)
            part_v[o, i, core] = total.astype(BF).reshape(n_r, share, width)

    def scatter(p, n):
        start, rows, order = parts[p]
        axis = order[2 - n]
        return [
            wire.copy(
                part_v.at[box(part_v, order[:2 - n], start, rows, core, (axis, to))],
                slots[3 * p + n].at[k - 1], d,
            )
            for k, to, d in peers(axis)
        ]

    def scatter_add(p, n, sent):
        start, rows, order = parts[p]
        at = box(part_v, order[:2 - n], start, rows, core)
        arrived(sent)
        total = part_v[at].astype(F32)
        for k in range(len(sent)):
            total = total + slots[3 * p + n][k].astype(F32)
        if n < 2:
            part_v[at] = total.astype(BF)
        else:
            fg_ref[start:start + rows, :] = (selfp[start:start + rows, :] + total).astype(BF)

    turns = rest[:1] + lead + rest[1:]
    sent = {p: scatter(p, 0) for p in every}

    arrived(grads + biases)
    total = g_v[core, chip].astype(F32)
    for k in range(1, n_c):
        total = total + g_chip[k - 1].astype(F32)
    g_rep[rep] = total.astype(BF)
    grads = [wire.copy(g_rep.at[rep], g_rep.at[rep], d) for _, _, d in peers("r")]
    b_rep[rep] = bias_sum_of(b_chip, n_c)
    biases = [wire.copy(b_rep.at[rep], b_rep.at[rep], d) for _, _, d in peers("r")]

    for p in turns:
        scatter_add(p, 0, sent[p])
        sent[p] = scatter(p, 1)

    arrived(grads + biases)
    total = g_rep[0].astype(F32)
    for k in range(1, n_r):
        total = total + g_rep[k].astype(F32)
    ga[core, chip] = total.astype(BF)
    grads = [wire.copy(ga.at[core, chip], ga.at[core, chip], d) for _, _, d in chips()]
    gb_ref[...] = jnp.broadcast_to(bias_sum_of(b_rep, n_r), (8, width))

    for p in turns:
        scatter_add(p, 1, sent[p])
        sent[p] = scatter(p, 2)

    arrived(grads)
    last = wire.copy(ga.at[core], ga.at[core], sibling)
    for p in turns:
        scatter_add(p, 2, sent[p])
    last.wait_recv()

    for c in wire.copies:
        c.wait_send()


def finish(hid_in, fg_in, ga, gb_in, hid_ref, fg_ref, gs_ref, gn_ref, gb_ref):
    width = gs_ref.shape[0]
    hid_ref[...] = hid_in[...]
    fg_ref[...] = fg_in[...]
    gs_ref[...] = ga[0].astype(F32).reshape(width, width)
    gn_ref[...] = ga[1].astype(F32).reshape(width, width)
    gb_ref[...] = gb_in[0:1, :].reshape(width)


def shards(n_blk, n_rep, features, degree, tiles, block_rows, block_cols, live, w_self, w_neigh, bias, cotangent):
    _, _, nslab, cap, tile, _ = tiles.shape
    slab, width = features.shape
    share = slab // n_rep
    n_i = 2
    n_o = n_blk // (2 * n_i)
    sizes = {"o": n_o, "i": n_i, "r": n_rep}
    parts = split_rows(share)
    n_c = n_o * n_i
    grows = width // n_c
    nodes = (n_o, n_i, 2, n_rep, share, width)
    ncopy = 8 + (len(parts) + 1) * 2 * (n_o + n_i + n_rep) + n_o + n_c * 3 + n_rep * 4
    vmem = pl.BlockSpec(memory_space=pltpu.VMEM)
    smem = pl.BlockSpec(memory_space=pltpu.SMEM)
    scratch = [
        pltpu.VMEM((nslab, cap, tile, tile), BF),
        pltpu.VMEM((nslab, slab, slab), BF),
        pltpu.VMEM((nslab, slab, slab), BF),
        pltpu.VMEM(nodes, BF),
        pltpu.VMEM(nodes, BF),
        pltpu.VMEM((share, width), F32),
        pltpu.VMEM((slab, 128), F32),
        pltpu.VMEM((width, share), BF),
        pltpu.VMEM((slab, width), F32),
        pltpu.VMEM((n_rep, share, width), BF),
        pltpu.VMEM((max(1, n_rep - 1), share, width), BF),
        pltpu.VMEM((n_rep, share, width), BF),
        pltpu.VMEM((n_o, n_i, n_rep, share, width), BF),
        pltpu.VMEM((share, width), F32),
        pltpu.VMEM((2, n_c, grows, width), BF),
        pltpu.VMEM((n_c, grows, width), BF),
        pltpu.VMEM((n_c - 1, grows, width), BF),
        pltpu.VMEM((n_rep, grows, width), BF),
        pltpu.VMEM((2, 1, width), F32),
        pltpu.VMEM((n_c, 1, width), F32),
        pltpu.VMEM((n_rep, 1, width), F32),
        pltpu.VMEM((width, width), BF),
        pltpu.VMEM((width, width), BF),
        pltpu.VMEM((slab, width), BF),
        pltpu.SemaphoreType.DMA((ncopy,)),
        pltpu.SemaphoreType.DMA((ncopy,)),
        pltpu.SemaphoreType.DMA((4,)),
    ] + [pltpu.VMEM(s, BF) for s in slot_shapes(parts, sizes, width)]
    anywhere = pl.BlockSpec(memory_space=pl.ANY)
    done = pl.pallas_call(
        functools.partial(kernel, sizes, parts, nslab, cap, tile, width, slab, share),
        out_shape=(
            jax.ShapeDtypeStruct((share, width), BF),
            jax.ShapeDtypeStruct((share, width), BF),
            jax.ShapeDtypeStruct((2, n_c, grows, width), BF),
            jax.ShapeDtypeStruct((8, width), F32),
        ),
        in_specs=[vmem, vmem, anywhere, smem, smem, smem, anywhere, anywhere, vmem, anywhere],
        out_specs=(vmem,) * 4,
        scratch_shapes=scratch,
        compiler_params=pltpu.CompilerParams(
            collective_id=0, has_side_effects=True, vmem_limit_bytes=56 * 1024 * 1024
        ),
        cost_estimate=pl.CostEstimate(
            flops=4 * slab * nslab * slab * width, bytes_accessed=2 * tiles.size, transcendentals=share * width
        ),
        name="sage_layer",
    )(features, degree, tiles, jnp.swapaxes(block_rows, 2, 3), jnp.swapaxes(block_cols, 2, 3), live, w_self, w_neigh, bias, cotangent)
    return pl.pallas_call(
        finish,
        out_shape=(
            jax.ShapeDtypeStruct((share, width), BF),
            jax.ShapeDtypeStruct((share, width), BF),
            jax.ShapeDtypeStruct((width, width), F32),
            jax.ShapeDtypeStruct((width, width), F32),
            jax.ShapeDtypeStruct((width,), F32),
        ),
        in_specs=[vmem] * 4,
        out_specs=(vmem,) * 5,
        name="write_results",
    )(*done)


def solution(mesh):
    n_blk, n_rep = mesh.shape["blk"], mesh.shape["rep"]
    return jax.shard_map(
        functools.partial(shards, n_blk, n_rep),
        mesh=mesh,
        in_specs=(
            P("blk", None),
            P("blk"),
            P("blk", "rep", None, None, None, None),
            P("blk", "rep", None, None),
            P("blk", "rep", None, None),
            P("blk", "rep", None),
            P(),
            P(),
            P(),
            P("blk", None),
        ),
        out_specs=(P(("blk", "rep"), None), P(("blk", "rep"), None), P(), P(), P()),
        check_vma=False,
    )
```

```python
import functools

import jax
import jax.numpy as jnp
from jax import lax
from jax.experimental import pallas as pl
from jax.experimental.pallas import tpu as pltpu
from jax.sharding import PartitionSpec as P

BF = jnp.bfloat16
F32 = jnp.float32
MESH = pl.DeviceIdType.MESH
NT = (((1,), (1,)), ((), ()))
ROWS = 16
STRIP = 32


def split_rows(share):
    units = share // ROWS
    side = max(1, units * 3 // 8)
    sizes = [side, units - 2 * side, side]
    orders = ["oir", "iro", "roi"]
    parts, at = [], 0
    for size, order in zip(sizes, orders):
        if size > 0:
            parts.append((at * ROWS, size * ROWS, order))
            at += size
    return parts


def slot_shapes(parts, sizes, width):
    shapes = []
    for _, rows, order in parts:
        left = dict(sizes)
        for axis in reversed(order):
            peers = left.pop(axis) - 1
            shapes.append((peers,) + tuple(left[a] for a in "oir" if a in left) + (rows, width))
    return shapes


class Wire:
    def __init__(self, send, recv):
        self.send, self.recv, self.copies = send, recv, []

    def copy(self, src, dst, device):
        k = len(self.copies)
        c = pltpu.make_async_remote_copy(
            src_ref=src, dst_ref=dst, send_sem=self.send.at[k], recv_sem=self.recv.at[k],
            device_id=device, device_id_type=MESH,
        )
        c.start()
        self.copies.append(c)
        return c


def kernel(
    sizes, parts, nslab, cap, tile, width, slab, share,
    x_ref, deg_ref, tiles_ref, rows_ref, cols_ref, live_ref, ws_hbm, wn_hbm, bias_ref, cot_hbm,
    hid_ref, fg_ref, ga, gb_ref,
    tv, a_v, at_v, xg, part_v, xw, degc, xt, aggp, aggs, aggr, dg, core_in, selfp,
    g_v, g_core, g_chip, g_rep, b_core, b_chip, b_rep, ws_v, wn_v, cot_v,
    send_sem, recv_sem, local_sem, *slots,
):
    n_o, n_i, n_r = sizes["o"], sizes["i"], sizes["r"]
    nb = slab // tile
    blk = lax.axis_index("blk")
    rep = lax.axis_index("rep")
    core = lax.rem(blk, 2)
    sib = 1 - core
    me = {"o": blk // (2 * n_i), "i": lax.rem(blk // 2, n_i), "r": rep}
    wire = Wire(send_sem, recv_sem)

    def device(axis, to):
        at = dict(me)
        at[axis] = to
        return ((at["o"] * n_i + at["i"]) * 2 + core, at["r"])

    sibling = ((me["o"] * n_i + me["i"]) * 2 + sib, rep)

    def peers(axis):
        for k in range(1, sizes[axis]):
            to = lax.rem(me[axis] + k, sizes[axis])
            yield k, to, device(axis, to)

    n_c = n_o * n_i
    chip = blk // 2

    def chips():
        for k in range(1, n_c):
            to = lax.rem(chip + k, n_c)
            yield k, to, (to * 2 + core, rep)

    loads = [
        pltpu.make_async_copy(src, dst, local_sem.at[k])
        for k, (src, dst) in enumerate(
            [(tiles_ref.at[0, 0], tv), (ws_hbm, ws_v), (wn_hbm, wn_v), (cot_hbm, cot_v)]
        )
    ]
    for c in loads:
        c.start()

    mine = pl.multiple_of(rep * share, share)
    x_mine = x_ref[pl.ds(mine, share), :]
    xg[me["o"], me["i"], core, rep] = x_mine
    for start, rows, order in parts:
        if order[0] == "r":
            for k in range(n_r):
                at = k * share + start
                xg[me["o"], me["i"], core, k, start:start + rows, :] = x_ref[at:at + rows, :]

    barrier = pltpu.get_barrier_semaphore()
    everyone = [sibling] + [d for _, _, d in chips()] + [d for _, _, d in peers("r")]
    for d in everyone:
        pl.semaphore_signal(barrier, inc=1, device_id=d, device_id_type=MESH)
    pl.semaphore_wait(barrier, len(everyone))

    def box(ref, have, start, rows, core_at, fixed=None):
        at = [slice(None) if a in have else me[a] for a in "oir"]
        if fixed is not None:
            at["oir".index(fixed[0])] = fixed[1]
        return (at[0], at[1], core_at, at[2], pl.ds(start, rows), slice(None))

    def gather(p, n):
        start, rows, order = parts[p]
        if n == 0 and order[0] == "r":
            return []
        if n == 3:
            at = box(xg, "oir", start, rows, core)
            return [wire.copy(xg.at[at], xg.at[at], sibling)]
        at = box(xg, order[:n], start, rows, core)
        return [wire.copy(xg.at[at], xg.at[at], d) for _, _, d in peers(order[n])]

    def arrived(copies):
        for c in copies:
            c.wait_recv()

    every = range(len(parts))
    lead = [p for p in every if parts[p][2][0] == "r"]
    rest = [p for p in every if p not in lead]

    flying = {p: gather(p, 1) for p in lead}
    for p in rest:
        flying[p] = gather(p, 0)

    loads[0].wait()

    def build(s, carry):
        live = live_ref[0, 0, s]
        weights = []
        for c in range(cap):
            row, col = rows_ref[0, 0, c, s], cols_ref[0, 0, c, s]
            used = c < live
            weights.append([
                [jnp.where(used & (row == i) & (col == j), 1.0, 0.0).astype(F32) for j in range(nb)]
                for i in range(nb)
            ])
        for r0 in range(0, tile, STRIP):
            acc = [[jnp.zeros((STRIP, tile), F32) for _ in range(nb)] for _ in range(nb)]
            for c in range(cap):
                t = tv[s, c, r0:r0 + STRIP, :].astype(F32)
                for i in range(nb):
                    for j in range(nb):
                        acc[i][j] = acc[i][j] + t * weights[c][i][j]
            for i in range(nb):
                for j in range(nb):
                    a_v[s, i * tile + r0:i * tile + r0 + STRIP, j * tile:(j + 1) * tile] = acc[i][j].astype(BF)
        at_v[s] = a_v[s].T
        return carry

    half = nslab // 2
    lax.fori_loop(0, half, build, 0)

    for p in reversed(rest):
        arrived(flying[p])
        flying[p] = gather(p, 1)

    lax.fori_loop(half, nslab, build, 0)
    for c in loads[1:]:
        c.wait()
    xw[...] = jnp.dot(x_mine, ws_v[...], preferred_element_type=F32)
    xt[...] = x_mine.T
    degf = deg_ref[...].astype(F32).reshape(1, slab)
    degc[...] = jnp.broadcast_to(degf, (128, slab)).T

    for p in list(reversed(rest)) + lead:
        arrived(flying[p])
        flying[p] = gather(p, 2)
    for p in rest[:1] + lead + rest[1:]:
        arrived(flying[p])
        flying[p] = gather(p, 3)

    def forward(core_at):
        acc = None
        for o in range(n_o):
            for i in range(n_i):
                s = (o * n_i + i) * 2 + core_at
                d = jnp.dot(a_v[s], xg[o, i, core_at].reshape(slab, width), preferred_element_type=F32)
                acc = d if acc is None else acc + d
        return acc

    aggp[...] = forward(core)
    for p in every:
        arrived(flying[p])
    aggp[...] = aggp[...] + forward(sib)

    aggs[...] = aggp[...].astype(BF).reshape(n_r, share, width)
    flying = [wire.copy(aggs.at[to], aggr.at[k - 1], d) for k, to, d in peers("r")]
    agg_sum = aggp[pl.ds(mine, share), :]
    for c in flying:
        c.wait_recv()
    for k in range(1, n_r):
        agg_sum = agg_sum + aggr[k - 1].astype(F32)
    degm = degc[pl.ds(mine, share), :]
    deg = jnp.concatenate([degm] * (width // 128), axis=1)
    agg = (agg_sum / deg).astype(BF)
    pre = xw[...] + jnp.dot(agg, wn_v[...], preferred_element_type=F32) + bias_ref[...].reshape(1, width)
    sig = jax.nn.sigmoid(pre)
    cot = cot_v[pl.ds(mine, share), :].astype(F32)
    dpre = (cot * (sig * (1.0 + pre * (1.0 - sig)))).astype(BF)
    dagg = lax.dot_general(dpre, wn_v[...], NT, preferred_element_type=F32) / deg
    dg[rep] = dagg.astype(BF)
    flying = [wire.copy(dg.at[rep], dg.at[rep], d) for _, _, d in peers("r")]

    hid_ref[...] = (pre * sig).astype(BF)
    piece = g_v.shape[1:-1]
    g_v[0] = jnp.dot(xt[...], dpre, preferred_element_type=F32).astype(BF).reshape(piece + (width,))
    g_v[1] = jnp.dot(agg.T, dpre, preferred_element_type=F32).astype(BF).reshape(piece + (width,))
    grads = [wire.copy(g_v.at[sib], g_core, sibling)]
    bias_sum = jnp.sum(dpre.astype(F32), axis=0, keepdims=True)
    b_core[core] = bias_sum
    biases = [wire.copy(b_core.at[core], b_core.at[core], sibling)]
    selfp[...] = lax.dot_general(dpre, ws_v[...], NT, preferred_element_type=F32)

    for c in flying:
        c.wait_recv()
    dgs = dg[...].reshape(slab, width)

    def backward(o, i, core_at):
        s = (o * n_i + i) * 2 + core_at
        return jnp.dot(at_v[s], dgs, preferred_element_type=F32)

    def bias_sum_of(b_ref, n):
        total = b_ref[0]
        for k in range(1, n):
            total = total + b_ref[k]
        return total

    arrived(grads + biases)
    g_v[core] = (g_v[core].astype(F32) + g_core[...].astype(F32)).astype(BF)
    grads = [wire.copy(g_v.at[core, to], g_chip.at[k - 1], d) for k, to, d in chips()]
    b_chip[chip] = bias_sum_of(b_core, 2)
    biases = [wire.copy(b_chip.at[chip], b_chip.at[chip], d) for _, _, d in chips()]

    across = []
    for o in range(n_o):
        for i in range(n_i):
            part_v[o, i, sib] = backward(o, i, sib).astype(BF).reshape(n_r, share, width)
        across.append(wire.copy(part_v.at[o, :, sib], core_in.at[o], sibling))

    for o in range(n_o):
        across[o].wait_recv()
        for i in range(n_i):
            total = backward(o, i, core) + core_in[o, i].astype(F32).reshape(slab, width)
            part_v[o, i, core] = total.astype(BF).reshape(n_r, share, width)

    def scatter(p, n):
        start, rows, order = parts[p]
        axis = order[2 - n]
        return [
            wire.copy(
                part_v.at[box(part_v, order[:2 - n], start, rows, core, (axis, to))],
                slots[3 * p + n].at[k - 1], d,
            )
            for k, to, d in peers(axis)
        ]

    def scatter_add(p, n, sent):
        start, rows, order = parts[p]
        at = box(part_v, order[:2 - n], start, rows, core)
        arrived(sent)
        total = part_v[at].astype(F32)
        for k in range(len(sent)):
            total = total + slots[3 * p + n][k].astype(F32)
        if n < 2:
            part_v[at] = total.astype(BF)
        else:
            fg_ref[start:start + rows, :] = (selfp[start:start + rows, :] + total).astype(BF)

    turns = rest[:1] + lead + rest[1:]
    sent = {p: scatter(p, 0) for p in every}

    arrived(grads + biases)
    total = g_v[core, chip].astype(F32)
    for k in range(1, n_c):
        total = total + g_chip[k - 1].astype(F32)
    g_rep[rep] = total.astype(BF)
    grads = [wire.copy(g_rep.at[rep], g_rep.at[rep], d) for _, _, d in peers("r")]
    b_rep[rep] = bias_sum_of(b_chip, n_c)
    biases = [wire.copy(b_rep.at[rep], b_rep.at[rep], d) for _, _, d in peers("r")]

    for p in turns:
        scatter_add(p, 0, sent[p])
        sent[p] = scatter(p, 1)

    arrived(grads + biases)
    total = g_rep[0].astype(F32)
    for k in range(1, n_r):
        total = total + g_rep[k].astype(F32)
    ga[core, chip] = total.astype(BF)
    grads = [wire.copy(ga.at[core, chip], ga.at[core, chip], d) for _, _, d in chips()]
    gb_ref[...] = jnp.broadcast_to(bias_sum_of(b_rep, n_r), (8, width))

    for p in turns:
        scatter_add(p, 1, sent[p])
        sent[p] = scatter(p, 2)

    arrived(grads)
    last = wire.copy(ga.at[core], ga.at[core], sibling)
    for p in turns:
        scatter_add(p, 2, sent[p])
    last.wait_recv()

    for c in wire.copies:
        c.wait_send()


def finish(hid_in, fg_in, ga, gb_in, hid_ref, fg_ref, gs_ref, gn_ref, gb_ref):
    width = gs_ref.shape[0]
    hid_ref[...] = hid_in[...]
    fg_ref[...] = fg_in[...]
    gs_ref[...] = ga[0].astype(F32).reshape(width, width)
    gn_ref[...] = ga[1].astype(F32).reshape(width, width)
    gb_ref[...] = gb_in[0:1, :].reshape(width)


def shards(n_blk, n_rep, features, degree, tiles, block_rows, block_cols, live, w_self, w_neigh, bias, cotangent):
    _, _, nslab, cap, tile, _ = tiles.shape
    slab, width = features.shape
    share = slab // n_rep
    n_i = 2
    n_o = n_blk // (2 * n_i)
    sizes = {"o": n_o, "i": n_i, "r": n_rep}
    parts = split_rows(share)
    n_c = n_o * n_i
    grows = width // n_c
    nodes = (n_o, n_i, 2, n_rep, share, width)
    ncopy = 8 + (len(parts) + 1) * 2 * (n_o + n_i + n_rep) + n_o + n_c * 3 + n_rep * 4
    vmem = pl.BlockSpec(memory_space=pltpu.VMEM)
    smem = pl.BlockSpec(memory_space=pltpu.SMEM)
    scratch = [
        pltpu.VMEM((nslab, cap, tile, tile), BF),
        pltpu.VMEM((nslab, slab, slab), BF),
        pltpu.VMEM((nslab, slab, slab), BF),
        pltpu.VMEM(nodes, BF),
        pltpu.VMEM(nodes, BF),
        pltpu.VMEM((share, width), F32),
        pltpu.VMEM((slab, 128), F32),
        pltpu.VMEM((width, share), BF),
        pltpu.VMEM((slab, width), F32),
        pltpu.VMEM((n_rep, share, width), BF),
        pltpu.VMEM((max(1, n_rep - 1), share, width), BF),
        pltpu.VMEM((n_rep, share, width), BF),
        pltpu.VMEM((n_o, n_i, n_rep, share, width), BF),
        pltpu.VMEM((share, width), F32),
        pltpu.VMEM((2, n_c, grows, width), BF),
        pltpu.VMEM((n_c, grows, width), BF),
        pltpu.VMEM((n_c - 1, grows, width), BF),
        pltpu.VMEM((n_rep, grows, width), BF),
        pltpu.VMEM((2, 1, width), F32),
        pltpu.VMEM((n_c, 1, width), F32),
        pltpu.VMEM((n_rep, 1, width), F32),
        pltpu.VMEM((width, width), BF),
        pltpu.VMEM((width, width), BF),
        pltpu.VMEM((slab, width), BF),
        pltpu.SemaphoreType.DMA((ncopy,)),
        pltpu.SemaphoreType.DMA((ncopy,)),
        pltpu.SemaphoreType.DMA((4,)),
    ] + [pltpu.VMEM(s, BF) for s in slot_shapes(parts, sizes, width)]
    anywhere = pl.BlockSpec(memory_space=pl.ANY)
    done = pl.pallas_call(
        functools.partial(kernel, sizes, parts, nslab, cap, tile, width, slab, share),
        out_shape=(
            jax.ShapeDtypeStruct((share, width), BF),
            jax.ShapeDtypeStruct((share, width), BF),
            jax.ShapeDtypeStruct((2, n_c, grows, width), BF),
            jax.ShapeDtypeStruct((8, width), F32),
        ),
        in_specs=[vmem, vmem, anywhere, smem, smem, smem, anywhere, anywhere, vmem, anywhere],
        out_specs=(vmem,) * 4,
        scratch_shapes=scratch,
        compiler_params=pltpu.CompilerParams(
            collective_id=0, has_side_effects=True, vmem_limit_bytes=56 * 1024 * 1024
        ),
        cost_estimate=pl.CostEstimate(
            flops=4 * slab * nslab * slab * width, bytes_accessed=2 * tiles.size, transcendentals=share * width
        ),
        name="sage_layer",
    )(features, degree, tiles, jnp.swapaxes(block_rows, 2, 3), jnp.swapaxes(block_cols, 2, 3), live, w_self, w_neigh, bias, cotangent)
    return pl.pallas_call(
        finish,
        out_shape=(
            jax.ShapeDtypeStruct((share, width), BF),
            jax.ShapeDtypeStruct((share, width), BF),
            jax.ShapeDtypeStruct((width, width), F32),
            jax.ShapeDtypeStruct((width, width), F32),
            jax.ShapeDtypeStruct((width,), F32),
        ),
        in_specs=[vmem] * 4,
        out_specs=(vmem,) * 5,
        name="write_results",
    )(*done)


def solution(mesh):
    n_blk, n_rep = mesh.shape["blk"], mesh.shape["rep"]
    return jax.shard_map(
        functools.partial(shards, n_blk, n_rep),
        mesh=mesh,
        in_specs=(
            P("blk", None),
            P("blk"),
            P("blk", "rep", None, None, None, None),
            P("blk", "rep", None, None),
            P("blk", "rep", None, None),
            P("blk", "rep", None),
            P(),
            P(),
            P(),
            P("blk", None),
        ),
        out_specs=(P(("blk", "rep"), None), P(("blk", "rep"), None), P(), P(), P()),
        check_vma=False,
    )
```
